512 devices in a mesh: ep: 128 (over z, y, core), dec: 4 (over x).
Axes of the slice: x: 4, y: 8, z: 8, core: 2. Of those that a mesh axis runs over, the one named last changes fastest.
Arguments:
- tokens: bfloat16 [8192, 3584], P('ep', 'dec')
- expert_ids: int32 [8192, 8], P('ep'), may hold values from 0 to 127, all different within a row; in each aligned block of 64 rows (0 to 63, 64 to 127, ...) at most 5 rows name the same one
- route_scores: float32 [8192, 8], P('ep'), may hold values from -6 to 6
- up_weight: bfloat16 [128, 3584, 1024], P('ep', 'dec'), may hold values from -0.09375 to 0.09375
- down_weight: bfloat16 [128, 1024, 3584], P('ep', None, 'dec'), may hold values from -0.1875 to 0.1875
- latent_weight: bfloat16 [3584, 576], P('dec')
- latent_norm_gain: float32 [512], replicated, may hold values from 0.5 to 1.5
- page_owner: int32 [512], P('ep'), may hold values from 0 to 3, as said below
Outputs:
- combined: bfloat16 [8192, 3584], P('ep', 'dec')
- kv_pages: bfloat16 [8192, 576], P(('ep', 'dec'))
The draws below stay inside these ranges and needn't reach their ends.
Inputs may be any that keep to these rules, and one draw needn't show every extreme that they name: `expert_ids`: each row names 8 different experts; among the 64 rows of one index of ep no expert is named by more than 5 rows, a bound that some block reaches. `page_owner`: within each aligned run of 4 pages every owner appears exactly 1 times.
All inputs are finite; a program needn't handle non-finite values.
Results may differ from the reference program's by a relative error of at most 0.02.
Values may be sent and summed in bfloat16 or wider, within the bound.
A program may use at most 64 MiB of HBM per device.

```python
import math
import jax
import jax.numpy as jnp
import numpy as np
from jax import lax

D = 3584
HID = 1024
LATENT_WIDTH = 512
PAGE = 16
TOK_DEV = 64
KV = 576
TOPK = 8
EXPERTS = 128
CAP = 5
TOKENS = 8192
PAGES_DEV = 4
OWN_PAGES = 1
N_DEC = 4


def draw_tokens(key, part):
    key = jax.random.fold_in(key, 11)
    key_values, key_scale = jax.random.split(key, 2)
    scales = jnp.exp(jax.random.uniform(key_scale, (TOKENS, 1), jnp.float32, math.log(0.3), math.log(3.0)))
    values = jnp.clip(jax.random.normal(key_values, (TOKENS, D), jnp.float32), -6.0, 6.0)
    return (values * scales).astype(jnp.bfloat16)


def draw_latent_weight(key, part):
    key = jax.random.fold_in(key, 17)
    key_values, key_scale = jax.random.split(key)
    columns = jnp.exp(jax.random.uniform(key_scale, (1, KV), jnp.float32, math.log(0.3), math.log(3.0)))
    values = jnp.clip(jax.random.normal(key_values, (D, KV), jnp.float32), -6.0, 6.0)
    return (values * columns / math.sqrt(D)).astype(jnp.bfloat16)


def draw_page_owner(key, part):
    key = jax.random.fold_in(key, 13)
    page_runs = TOKENS // PAGE // PAGES_DEV
    scores = jax.random.randint(key, (page_runs, PAGES_DEV), 0, 1 << 20) * PAGES_DEV
    scores = scores + jnp.arange(PAGES_DEV, dtype=jnp.int32)[None, :]
    ranking = jnp.argsort(jnp.argsort(scores, axis=1), axis=1)
    return (ranking // OWN_PAGES).reshape(-1).astype(jnp.int32)


def steps_of(stream_key, extent, shards, least, high):
    def one(axis_at, blocks):
        heights = jax.random.uniform(jax.random.fold_in(jax.random.fold_in(stream_key, 6), axis_at), (blocks,), jnp.float32, least / len(shards), high / len(shards))
        return jnp.repeat(jnp.exp(heights), extent[axis_at] // blocks).reshape((-1,) + (1,) * (len(extent) - axis_at - 1))

    gain = one(*shards[0])
    for cut in shards[1:]:
        gain = gain * one(*cut)
    return gain


def deal_out(key, own, number, rows, count, top, bound, slope):
    order = jax.random.permutation(key, count)
    crowded, usual = portions_of(count, rows * top, bound, slope, True), portions_of(count, rows * top, bound, slope, False)
    places = jnp.arange(count)

    def named(lengths, turn):
        used = int((lengths > 0).sum())
        fixed = max(1, used // 4)
        moved = fixed + (places - fixed + turn * (used - fixed)) % max(1, count - fixed)
        return jnp.zeros((count,), jnp.int32).at[order[jnp.where(places < fixed, places, moved)]].set(jnp.asarray(lengths, jnp.int32))

    lengths = jnp.where(number % 4 == 0, named(crowded, number // 4), named(usual, number - number // 4 - 1))
    mixed = jax.random.permutation(jax.random.fold_in(own, 3), count)
    source_of, taker = mixed[0:count // 2 * 2:2], mixed[1:count // 2 * 2:2]
    room = jnp.minimum(lengths[source_of] - 1, bound - lengths[taker]) // 2
    room = jnp.where((source_of == order[0]) | (taker == order[0]) | (lengths[taker] == 0), 0, jnp.maximum(room, 0))
    moved = jax.random.randint(jax.random.fold_in(own, 4), (count // 2,), 0, 1 << 20) % (room + 1)
    lengths = lengths.at[source_of].add(-moved).at[taker].add(moved)
    members = jnp.searchsorted(jnp.cumsum(lengths), jnp.arange(rows * top), side="right").astype(jnp.int32)
    grid = members.reshape(top, rows).T
    grid = grid[jax.random.permutation(jax.random.fold_in(own, 1), rows)]
    turn = jax.random.randint(jax.random.fold_in(own, 2), (rows, 1), 0, top)
    return jnp.take_along_axis(grid, (jnp.arange(top)[None, :] + turn) % top, axis=1)


def portions_of(count, total, reach, slope, full):
    weights = [(1 << 20) // math.isqrt(grade ** slope) + 1 for grade in range(1, count + 1)]
    largest = reach if full else min(reach, max(-(-total // count), total * weights[0] // sum(weights)))
    least = 1 if total - largest >= count - 1 else 0
    counts, rest = [largest] + [least] * (count - 1), total - largest - least * (count - 1)
    while rest > 0:
        movable = [i for i in range(1, count) if counts[i] < largest] or [i for i in range(1, count) if counts[i] < reach]
        whole, remaining = sum([weights[i] for i in movable]), rest
        for i in movable:
            extra = min(reach - counts[i], max(1, remaining * weights[i] // whole), rest)
            counts[i] = counts[i] + extra
            rest = rest - extra
    return np.array(counts)


def noise(rng, extent, deviation, bound, shards=(), held_as=jnp.bfloat16):
    result = jax.random.normal(rng, extent, jnp.float32) * deviation
    if len(shards) > 0:
        result = steps_of(rng, extent, shards, -0.22, 0.18) * result
    return jnp.clip(result, min=-bound, max=bound).astype(held_as)


def setup_inputs(seed: int = 0) -> dict:
    keys = jax.random.split(jax.random.key(seed), 9)
    tokens = draw_tokens(jax.random.fold_in(keys[8], 71), 0)
    expert_ids_keys = jax.random.split(jax.random.fold_in(keys[1], 1), TOKENS // TOK_DEV)
    expert_ids_turns = jax.random.permutation(jax.random.fold_in(keys[1], 3), TOKENS // TOK_DEV)
    expert_ids = jax.vmap(lambda own, number: deal_out(jax.random.fold_in(keys[1], 2), own, number, TOK_DEV, EXPERTS, TOPK, CAP, 2))(expert_ids_keys, expert_ids_turns).reshape((TOKENS, TOPK))
    route_scores = noise(keys[2], (TOKENS, TOPK), 1.5, 6.0, ((0, 128),), jnp.float32)
    up_weight = noise(keys[3], (EXPERTS, D, HID), D ** -0.5, 0.09375, ((0, 128), (1, 4)))
    down_weight = noise(keys[4], (EXPERTS, HID, D), HID ** -0.5, 0.1875, ((0, 128), (2, 4)))
    latent_weight = draw_latent_weight(jax.random.fold_in(keys[8], 71), 0)
    latent_norm_gain = jnp.clip(1.0 + 0.1 * jax.random.normal(keys[6], (LATENT_WIDTH,), jnp.float32), 0.5, 1.5)
    page_owner = draw_page_owner(jax.random.fold_in(keys[8], 71), 0)
    return {"tokens": tokens, "expert_ids": expert_ids, "route_scores": route_scores, "up_weight": up_weight, "down_weight": down_weight, "latent_weight": latent_weight, "latent_norm_gain": latent_norm_gain, "page_owner": page_owner}


route_scale = 2.5

def finish_rows(latent_rows, positions, norm_gain):
    latent_rank_width = norm_gain.shape[0]
    compressed_latent = latent_rows[:, :latent_rank_width]
    inverse_rms = lax.rsqrt(lax.optimization_barrier(jnp.mean(compressed_latent * compressed_latent, axis=1, keepdims=True)) + 1e-06)
    normed = compressed_latent * inverse_rms * norm_gain[None, :]
    half_rotary_width = (latent_rows.shape[1] - latent_rank_width) // 2
    frequency = jnp.power(10000.0, -jnp.arange(half_rotary_width, dtype=jnp.float32) * 2.0 / (2 * half_rotary_width))
    angles = positions[:, None] * frequency[None, :]
    cosine = jnp.cos(angles)
    sine_part = jnp.sin(angles)
    rotary_first_half = latent_rows[:, latent_rank_width:latent_rank_width + half_rotary_width]
    rotary_second_half = latent_rows[:, latent_rank_width + half_rotary_width:]
    rotated_first = rotary_first_half * cosine - rotary_second_half * sine_part
    rotated_second = rotary_second_half * cosine + rotary_first_half * sine_part
    return jnp.concatenate([normed, rotated_first, rotated_second], axis=1).astype(jnp.bfloat16)

def reference(tokens, expert_ids, route_scores, up_weight, down_weight, latent_weight, latent_norm_gain, page_owner):
    total_tokens, width = tokens.shape
    top_count = expert_ids.shape[1]
    experts = up_weight.shape[0]
    run_count = total_tokens // TOK_DEV
    gate_value = jax.nn.sigmoid(route_scores)
    route_weight = route_scale * gate_value / lax.optimization_barrier(jnp.sum(gate_value, axis=1, keepdims=True))
    flat_ids = expert_ids.reshape(run_count, TOK_DEV * top_count)
    expert_hits = (flat_ids[:, :, None] == jnp.arange(experts, dtype=jnp.int32)[None, None, :]).astype(jnp.int32)
    before = jnp.cumsum(expert_hits, axis=1) - expert_hits
    slot_rank = lax.optimization_barrier(jnp.sum(before * expert_hits, axis=2))
    slot_dest = flat_ids * CAP + slot_rank
    token_of = (jnp.arange(total_tokens * top_count, dtype=jnp.int32) // top_count).reshape(run_count, TOK_DEV * top_count)
    run_index = jnp.arange(run_count, dtype=jnp.int32)[:, None]
    slot_token = jnp.full((run_count, experts * CAP), total_tokens, jnp.int32).at[run_index, slot_dest].set(token_of)
    slot_weight = jnp.zeros((run_count, experts * CAP), jnp.float32).at[run_index, slot_dest].set(route_weight.reshape(run_count, TOK_DEV * top_count))
    slot_token = jnp.transpose(slot_token.reshape(run_count, experts, CAP), (1, 0, 2)).reshape(experts, run_count * CAP)
    slot_weight = jnp.transpose(slot_weight.reshape(run_count, experts, CAP), (1, 0, 2)).reshape(experts, run_count * CAP)
    quarter = width // N_DEC

    def expert_step(carry_rows, inputs):
        expert_tokens, expert_weights, up_matrix, down_matrix = inputs
        row_block = jnp.take(tokens, jnp.minimum(expert_tokens, total_tokens - 1), axis=0)
        row_count = row_block.shape[0]
        pieces = row_block.astype(jnp.float32).reshape(row_count, N_DEC, quarter)
        up_pieces = up_matrix.astype(jnp.float32).reshape(N_DEC, quarter, HID)
        partial_sums = jnp.einsum('rjd,jdh->rjh', pieces, up_pieces)
        partial_sums = lax.optimization_barrier(partial_sums.astype(jnp.bfloat16)).astype(jnp.float32)
        pre_act = lax.optimization_barrier(jnp.sum(partial_sums, axis=1))
        hidden = jax.nn.silu(pre_act).astype(jnp.bfloat16)
        expert_out = jnp.dot(hidden, down_matrix, preferred_element_type=jnp.float32).astype(jnp.bfloat16)
        carry_rows = carry_rows.at[expert_tokens].add(expert_weights[:, None] * expert_out.astype(jnp.float32), mode='drop')
        return (carry_rows, None)
    combined, _ = lax.scan(expert_step, jnp.zeros((total_tokens, width), jnp.float32), (slot_token, slot_weight, up_weight, down_weight))
    latent_rows = jnp.dot(tokens, latent_weight, preferred_element_type=jnp.float32)
    positions = jnp.arange(total_tokens, dtype=jnp.int32).astype(jnp.float32)
    kv_rows = finish_rows(latent_rows, positions, latent_norm_gain)
    page_total = total_tokens // PAGE
    page_index = jnp.arange(page_total, dtype=jnp.int32)
    sort_keys = (page_index // PAGES_DEV * N_DEC + page_owner) * page_total + page_index
    page_order = jnp.argsort(sort_keys).astype(jnp.int32)
    token_order = (page_order[:, None] * PAGE + jnp.arange(PAGE, dtype=jnp.int32)[None, :]).reshape(-1)
    kv_pages = jnp.take(kv_rows, token_order, axis=0)
    return (combined.astype(jnp.bfloat16), kv_pages)
```

```python
import functools

import jax
import jax.numpy as jnp
import numpy as np
from jax import lax
from jax.experimental import pallas as pl
from jax.experimental.pallas import tpu as pltpu
from jax.sharding import PartitionSpec as P

MESH = pl.DeviceIdType.MESH
bf16 = jnp.bfloat16
f32 = jnp.float32

ROUTE_SCALE = 2.5
N = 8
TOK = 64
TOP = 8
CAP = 5
MSG = N * CAP
QUARTER = 896
HID = 1024
LATENT = 512
KV = 576
PAGE = 16
PACK = 2304
CHUNKS = ((0, 1), (7, 2), (6, 3), (5, 4))
ROWS = 4 * MSG


def dot(a, b):
    return jnp.dot(a, b, preferred_element_type=f32)


def pack(ref, at, rows):
    ref[at, :, 0:QUARTER] = rows[0:16].astype(bf16)
    ref[at, :, QUARTER : 2 * QUARTER] = rows[16:32].astype(bf16)
    tail = rows[32:40]
    rest = jnp.concatenate([tail[:, 512:QUARTER], jnp.zeros((8, 128), f32)], axis=1)
    ref[at, :, 2 * QUARTER : PACK] = jnp.concatenate([tail[:, 0:512], rest], axis=0).astype(bf16)


def pack_pair(ref, first, second, rows):
    pack(ref, first, jnp.concatenate([rows[0:32], rows[64:72]], axis=0))
    pack(ref, second, jnp.concatenate([rows[32:64], rows[72:80]], axis=0))


def unpack_pair(ref, first, second):
    heads, tails = [], []
    for at in (first, second):
        heads += [ref[at, :, 0:QUARTER], ref[at, :, QUARTER : 2 * QUARTER]]
        tail = ref[at, :, 2 * QUARTER : PACK].astype(f32)
        tails.append(jnp.concatenate([tail[0:8], tail[8:16, 0 : QUARTER - 512]], axis=1))
    tail = jnp.concatenate(tails, axis=0).astype(bf16)
    return jnp.concatenate(heads + [tail], axis=0)


def kernel(
    tok_ref,
    ids_ref,
    scores_ref,
    up_hbm,
    down_hbm,
    lat_hbm,
    gain_ref,
    owner_ref,
    freq_ref,
    out_ref,
    kv_ref,
    up_ref,
    down_ref,
    lat_ref,
    line_tok,
    line_meta,
    code_ref,
    wsel_ref,
    disp_out,
    disp_in,
    back_out,
    back_in,
    chain_out,
    chain_in,
    part_ref,
    full_out,
    full_in,
    hid_ref,
    pick_ref,
    sum_ref,
    line_out,
    line_in,
    lat_out,
    lat_own,
    lat_in,
    load_sem,
    tok_send,
    tok_recv,
    meta_send,
    meta_recv,
    disp_send,
    disp_recv,
    back_send,
    back_recv,
    chain_send,
    chain_recv,
    full_send,
    full_recv,
    hid_send,
    hid_recv,
    line_send,
    line_recv,
    lat_send,
    lat_recv,
):
    ep = lax.axis_index("ep")
    x = lax.axis_index("dec")
    core = lax.rem(ep, 2)
    chip = lax.div(ep, 2)
    z = lax.div(chip, N)
    y = lax.rem(chip, N)
    on_z = core == 0
    mine = jnp.where(on_z, z, y)
    cross = jnp.where(on_z, y, z)

    def wrap(v):
        return lax.rem(v + 2 * N, N)

    def line_dev(step):
        place = wrap(mine + step)
        zz = jnp.where(on_z, place, z)
        yy = jnp.where(on_z, y, place)
        return ((zz * N + yy) * 2 + core, x)

    def expert_dev(step, c):
        place = wrap(cross + step)
        zz = jnp.where(on_z, z, place)
        yy = jnp.where(on_z, place, y)
        return ((zz * N + yy) * 2 + c, x)

    def source_dev(c_src, step):
        if c_src == 0:
            return ((z * N + wrap(y - step)) * 2, x)
        return ((wrap(z - step) * N + y) * 2 + 1, x)

    def dec_dev(step):
        return (ep, lax.rem(x + step + 4, 4))

    sent = []

    def send(src, dst, s_sem, r_sem, dev):
        copy = pltpu.make_async_remote_copy(
            src_ref=src, dst_ref=dst, send_sem=s_sem, recv_sem=r_sem, device_id=dev, device_id_type=MESH
        )
        copy.start()
        sent.append(copy)

    def arrived(dst, sem):
        pltpu.make_async_copy(dst, dst, sem).wait()

    loads = [
        pltpu.make_async_copy(lat_hbm, lat_ref, load_sem.at[0]),
        pltpu.make_async_copy(up_hbm.at[0], up_ref, load_sem.at[1]),
        pltpu.make_async_copy(down_hbm.at[0], down_ref, load_sem.at[2]),
    ]
    for load in loads:
        load.start()

    barrier = pltpu.get_barrier_semaphore()

    def greet(dev):
        pl.semaphore_signal(barrier, inc=1, device_id=dev, device_id_type=MESH)

    greet(((z * N + y) * 2 + 1 - core, x))
    for step in range(1, N):
        for c in range(2):
            greet(((z * N + wrap(y + step)) * 2 + c, x))
            greet(((wrap(z + step) * N + y) * 2 + c, x))
    for step in range(1, 4):
        greet(dec_dev(step))

    gate = jax.nn.sigmoid(scores_ref[...])
    weight = ROUTE_SCALE * gate / jnp.sum(gate, axis=1, keepdims=True)
    line_meta[0] = jnp.concatenate([ids_ref[...].astype(f32).T, weight.T], axis=1)
    line_tok[0] = tok_ref[...]

    lane = lax.broadcasted_iota(jnp.int32, (TOK, TOK), 1)
    row = lax.broadcasted_iota(jnp.int32, (TOK, TOK), 0)
    owner_of = jnp.zeros((TOK, TOK), jnp.int32)
    page = jnp.int32(0)
    for p in range(4):
        owner_of = jnp.where((lane >> 4) == p, owner_ref[p], owner_of)
        page = page + jnp.where(owner_ref[p] == x, p, 0)
    wanted = lax.rem((row >> 4) + x, 4)
    order = jnp.where((owner_of == wanted) & ((lane & 15) == (row & 15)), 1.0, 0.0).astype(bf16)
    ordered = dot(order, tok_ref[...]).astype(bf16)
    loads[0].wait()
    latent = dot(ordered, lat_ref[...])
    lat_own[...] = latent[0:PAGE]
    lat_out[...] = latent[PAGE:].astype(bf16).reshape(3, PAGE, KV)

    pl.semaphore_wait(barrier, 4 * (N - 1) + 4)

    def pass_on(k, h, plus):
        at = (2 * (k - 1) + h) if k < 4 else 6
        at = at if plus else 7 + at
        rows = pl.ds(h * 32, 32)
        slot = k if plus else N - k
        prev = k - 1 if plus else (N - k + 1) % N
        src = tok_ref.at[rows] if k == 1 else line_tok.at[prev, rows]
        send(src, line_tok.at[slot, rows], tok_send.at[at], tok_recv.at[at], line_dev(1 if plus else -1))

    def taken(k, h, plus):
        at = (2 * (k - 1) + h) if k < 4 else 6
        at = at if plus else 7 + at
        arrived(line_tok.at[k if plus else N - k, pl.ds(h * 32, 32)], tok_recv.at[at])

    for h in range(2):
        for plus in (True, False):
            pass_on(1, h, plus)
    for step in range(1, N):
        send(line_meta.at[0], line_meta.at[step], meta_send.at[step - 1], meta_recv.at[step - 1], line_dev(step))
    for step in range(1, 4):
        send(lat_out.at[step - 1], lat_in.at[step - 1], lat_send.at[step - 1], lat_recv.at[step - 1], dec_dev(step))
    for k in range(1, 4):
        for h in range(2):
            for plus in (True, False):
                taken(k, h, plus)
                if k < 3 or h == (0 if plus else 1):
                    pass_on(k + 1, h, plus)

    for step in range(1, N):
        arrived(line_meta.at[step], meta_recv.at[step - 1])
    low = lax.broadcasted_iota(jnp.int32, (TOP, 128), 1) < TOK
    ids, weights = [], []
    for pair in range(4):
        even, odd = line_meta[2 * pair], line_meta[2 * pair + 1]
        ids.append(jnp.where(low, even, pltpu.roll(odd, TOK, 1)))
        weights.append(jnp.where(low, pltpu.roll(even, TOK, 1), odd))
    ids = jnp.concatenate(ids, axis=1)
    weights = jnp.concatenate(weights, axis=1)
    number = lax.broadcasted_iota(jnp.int32, (16, 512), 0)
    place = lax.rem(cross + (number >> 1), N)
    expert = jnp.where(on_z, 16 * mine + 2 * place, 16 * place + 2 * mine) + (number & 1)
    expert = expert.astype(f32)
    hits = jnp.zeros((16, 512), f32)
    wsel = jnp.zeros((16, 512), f32)
    for k in range(TOP):
        match = ids[k : k + 1, :] == expert
        hits = jnp.where(match, 1.0, hits)
        wsel = jnp.where(match, weights[k : k + 1, :], wsel)
    before_r = lax.broadcasted_iota(jnp.int32, (128, 128), 0)
    before_c = lax.broadcasted_iota(jnp.int32, (128, 128), 1)
    before = jnp.where((before_r < before_c) & ((before_r >> 6) == (before_c >> 6)), 1.0, 0.0).astype(bf16)
    rank = jnp.concatenate(
        [dot(hits[:, 128 * i : 128 * i + 128].astype(bf16), before) for i in range(4)], axis=1
    )
    code_ref[...] = jnp.where(hits > 0.5, rank, -1.0)
    wsel_ref[...] = wsel

    slot_row = lax.broadcasted_iota(jnp.int32, (MSG, 512), 0)
    slot_lane = lax.broadcasted_iota(jnp.int32, (MSG, 512), 1)
    pattern = jnp.where((slot_lane >> 6) == (slot_row & 7), slot_row >> 3, -2).astype(f32)

    def picks(step, weighted):
        parts = []
        for c in range(2):
            at = 2 * step + c
            value = wsel_ref[at : at + 1, :] if weighted else 1.0
            parts.append(jnp.where(code_ref[at : at + 1, :] == pattern, value, 0.0))
        a, b = parts
        return jnp.concatenate([a[0:32], b[0:32], a[32:40], b[32:40]], axis=0)

    for h, plus in ((0, True), (1, False)):
        taken(4, h, plus)

    local = []
    for step in [s for chunk in CHUNKS for s in chunk]:
        rows = dot(picks(step, False).astype(bf16), line_tok[...].reshape(N * TOK, QUARTER))
        pack_pair(disp_out, 2 * step, 2 * step + 1, rows)
        slot = N * core + step
        if step == 0:
            copy = pltpu.make_async_copy(disp_out.at[core], disp_in.at[slot], disp_recv.at[slot])
            copy.start()
            other = 1 - core
            send(disp_out.at[other], disp_in.at[slot], disp_send.at[other], disp_recv.at[slot], expert_dev(0, other))
        else:
            for c in range(2):
                at = 2 * step + c
                send(disp_out.at[at], disp_in.at[slot], disp_send.at[at], disp_recv.at[slot], expert_dev(step, c))

    for j, chunk in enumerate(CHUNKS):
        both = jnp.concatenate([picks(step, True) for step in chunk], axis=0)
        pick_ref[j] = both.T.astype(bf16)

    for step in range(1, 4):
        arrived(lat_in.at[step - 1], lat_recv.at[step - 1])
    total = lat_own[...]
    for step in range(3):
        total = total + lat_in[step].astype(f32)
    comp = total[:, 0:LATENT]
    scale = lax.rsqrt(jnp.sum(comp * comp, axis=1, keepdims=True) * (1.0 / LATENT) + 1e-6)
    kv_ref[:, 0:LATENT] = (comp * scale * gain_ref[...]).astype(bf16)
    half = (KV - LATENT) // 2
    first, second = total[:, LATENT : LATENT + half], total[:, LATENT + half :]
    token = (ep * TOK + page * PAGE + lax.broadcasted_iota(jnp.int32, (PAGE, half), 0)).astype(f32)
    angle = token * freq_ref[...]
    cos, sin = jnp.cos(angle), jnp.sin(angle)
    kv_ref[:, LATENT:] = jnp.concatenate(
        [first * cos - second * sin, second * cos + first * sin], axis=1
    ).astype(bf16)

    loads[1].wait()
    loads[2].wait()

    def quarter_of(step):
        return pl.ds(pl.multiple_of(lax.rem(x + step + 4, 4) * 256, 256), 256)

    def stage_up(j):
        for step in CHUNKS[j]:
            for c in range(2):
                arrived(disp_in.at[N * c + step], disp_recv.at[N * c + step])
        block = jnp.concatenate([unpack_pair(disp_in, step, N + step) for step in CHUNKS[j]], axis=0)
        part = dot(block, up_ref[:, quarter_of(2)])
        for d in range(2):
            chain_out[j, d] = part[:, 128 * d : 128 * d + 128].astype(bf16)
            at = 2 * j + d
            send(
                chain_out.at[j, d],
                chain_in.at[j, d],
                chain_send.at[at],
                chain_recv.at[at],
                dec_dev(1 if d == 0 else -1),
            )
        part_ref[j, 0] = dot(block, up_ref[:, quarter_of(1)])
        part_ref[j, 1] = dot(block, up_ref[:, quarter_of(-1)])
        part_ref[j, 2] = dot(block, up_ref[:, quarter_of(0)])

    def stage_chain(j):
        for d in range(2):
            at = 2 * j + d
            arrived(chain_in.at[j, d], chain_recv.at[at])
            for half in range(2):
                value = part_ref[j, d, :, 128 * half : 128 * half + 128]
                if half == d:
                    value = value + chain_in[j, d].astype(f32)
                full_out[j, d, half] = value.astype(bf16)
            send(
                full_out.at[j, d],
                full_in.at[j, d],
                full_send.at[at],
                full_recv.at[at],
                dec_dev(1 if d == 0 else -1),
            )

    def stage_hidden(j):
        for d in range(2):
            arrived(full_in.at[j, d], full_recv.at[2 * j + d])
        for half in range(2):
            pre = part_ref[j, 2, :, 128 * half : 128 * half + 128]
            pre = pre + full_in[j, 0, half].astype(f32) + full_in[j, 1, half].astype(f32)
            hid_ref[j, 0, half] = (pre / (1.0 + jnp.exp(-pre))).astype(bf16)
        for d in range(2):
            send(
                hid_ref.at[j, 0],
                hid_ref.at[j, 1 + d],
                hid_send.at[4 * j + d],
                hid_recv.at[4 * j + d],
                dec_dev(1 if d == 0 else -1),
            )

    def stage_pass(j):
        for d in range(2):
            arrived(hid_ref.at[j, 1 + d], hid_recv.at[4 * j + d])
            send(
                hid_ref.at[j, 1 + d, d],
                hid_ref.at[j, 3, d],
                hid_send.at[4 * j + 2 + d],
                hid_recv.at[4 * j + 2 + d],
                dec_dev(1 if d == 0 else -1),
            )

    def stage_down(j):
        total = None
        for place, step in ((0, 0), (1, -1), (2, 1), (3, 2)):
            if place == 3:
                for d in range(2):
                    arrived(hid_ref.at[j, 3, d], hid_recv.at[4 * j + 2 + d])
            hidden = jnp.concatenate([hid_ref[j, place, 0], hid_ref[j, place, 1]], axis=1)
            term = dot(hidden, down_ref[quarter_of(step), :])
            total = term if total is None else total + term
        for i, step in enumerate(CHUNKS[j]):
            pack_pair(back_out, step, N + step, total[2 * MSG * i : 2 * MSG * (i + 1)])
            slot = 2 * step + core
            for c in range(2):
                at = N * c + step
                if step:
                    send(back_out.at[at], back_in.at[slot], back_send.at[at], back_recv.at[slot], source_dev(c, step))
            if step == 0:
                own, other = N * core, N * (1 - core)
                pltpu.make_async_copy(back_out.at[own], back_in.at[core], back_recv.at[core]).start()
                send(
                    back_out.at[other],
                    back_in.at[core],
                    back_send.at[other],
                    back_recv.at[core],
                    ((z * N + y) * 2 + 1 - core, x),
                )

    def stage_sum(j):
        for step in CHUNKS[j]:
            for c in range(2):
                arrived(back_in.at[2 * step + c], back_recv.at[2 * step + c])
        block = jnp.concatenate([unpack_pair(back_in, 2 * step, 2 * step + 1) for step in CHUNKS[j]], axis=0)
        term = dot(pick_ref[j], block)
        if j == 0:
            sum_ref[...] = term
        else:
            sum_ref[...] = sum_ref[...] + term

    stage_up(0)
    stage_chain(0)
    stage_up(1)
    stage_hidden(0)
    stage_chain(1)
    stage_pass(0)
    stage_up(2)
    stage_hidden(1)
    stage_chain(2)
    stage_down(0)
    stage_pass(1)
    stage_up(3)
    stage_hidden(2)
    stage_chain(3)
    stage_down(1)
    stage_pass(2)
    stage_hidden(3)
    stage_sum(0)
    stage_down(2)
    stage_pass(3)
    stage_sum(1)
    stage_down(3)
    stage_sum(2)
    stage_sum(3)

    for step in range(1, N):
        line_out[step - 1] = sum_ref[step * TOK : (step + 1) * TOK].astype(bf16)
        send(line_out.at[step - 1], line_in.at[step - 1], line_send.at[step - 1], line_recv.at[step - 1], line_dev(-step))
    total = sum_ref[0:TOK]
    for step in range(1, N):
        arrived(line_in.at[step - 1], line_recv.at[step - 1])
        total = total + line_in[step - 1].astype(f32)
    out_ref[...] = total.astype(bf16)

    for copy in sent:
        copy.wait_send()


def on_device(tokens, expert_ids, route_scores, up_weight, down_weight, latent_weight, latent_norm_gain, page_owner):
    half = (KV - LATENT) // 2
    freq = np.power(10000.0, -np.arange(half, dtype=np.float64) / half).astype(np.float32)
    vmem = pl.BlockSpec(memory_space=pltpu.VMEM)
    hbm = pl.BlockSpec(memory_space=pl.ANY)
    smem = pl.BlockSpec(memory_space=pltpu.SMEM)
    dma = pltpu.SemaphoreType.DMA
    return pl.pallas_call(
        kernel,
        out_shape=(
            jax.ShapeDtypeStruct((TOK, QUARTER), bf16),
            jax.ShapeDtypeStruct((PAGE, KV), bf16),
        ),
        in_specs=[vmem, vmem, vmem, hbm, hbm, hbm, vmem, smem, vmem],
        out_specs=(vmem, vmem),
        scratch_shapes=[
            pltpu.VMEM((QUARTER, HID), bf16),
            pltpu.VMEM((HID, QUARTER), bf16),
            pltpu.VMEM((QUARTER, KV), bf16),
            pltpu.VMEM((N, TOK, QUARTER), bf16),
            pltpu.VMEM((N, TOP, 128), f32),
            pltpu.VMEM((16, 512), f32),
            pltpu.VMEM((16, 512), f32),
            pltpu.VMEM((16, 16, PACK), bf16),
            pltpu.VMEM((16, 16, PACK), bf16),
            pltpu.VMEM((16, 16, PACK), bf16),
            pltpu.VMEM((16, 16, PACK), bf16),
            pltpu.VMEM((4, 2, ROWS, 128), bf16),
            pltpu.VMEM((4, 2, ROWS, 128), bf16),
            pltpu.VMEM((4, 3, ROWS, 256), f32),
            pltpu.VMEM((4, 2, 2, ROWS, 128), bf16),
            pltpu.VMEM((4, 2, 2, ROWS, 128), bf16),
            pltpu.VMEM((4, 4, 2, ROWS, 128), bf16),
            pltpu.VMEM((4, N * TOK, ROWS), bf16),
            pltpu.VMEM((N * TOK, QUARTER), f32),
            pltpu.VMEM((7, TOK, QUARTER), bf16),
            pltpu.VMEM((7, TOK, QUARTER), bf16),
            pltpu.VMEM((3, PAGE, KV), bf16),
            pltpu.VMEM((PAGE, KV), f32),
            pltpu.VMEM((3, PAGE, KV), bf16),
            dma((3,)),
            dma((14,)),
            dma((14,)),
            dma((7,)),
            dma((7,)),
            dma((16,)),
            dma((16,)),
            dma((16,)),
            dma((16,)),
            dma((8,)),
            dma((8,)),
            dma((8,)),
            dma((8,)),
            dma((16,)),
            dma((16,)),
            dma((7,)),
            dma((7,)),
            dma((3,)),
            dma((3,)),
        ],
        compiler_params=pltpu.CompilerParams(
            collective_id=0, has_side_effects=True, vmem_limit_bytes=40 * 1024 * 1024
        ),
    )(
        tokens,
        expert_ids,
        route_scores,
        up_weight,
        down_weight,
        latent_weight,
        latent_norm_gain.reshape(1, LATENT),
        page_owner,
        jnp.asarray(freq).reshape(1, half),
    )


def solution(mesh):
    placed = (
        P("ep", "dec"),
        P("ep", None),
        P("ep", None),
        P("ep", "dec", None),
        P("ep", None, "dec"),
        P("dec", None),
        P(),
        P("ep"),
    )
    return jax.shard_map(
        on_device,
        mesh=mesh,
        in_specs=placed,
        out_specs=(P("ep", "dec"), P(("ep", "dec"), None)),
        check_vma=False,
    )
```

```python
import functools

import jax
import jax.numpy as jnp
import numpy as np
from jax import lax
from jax.experimental import pallas as pl
from jax.experimental.pallas import tpu as pltpu
from jax.sharding import PartitionSpec as P

MESH = pl.DeviceIdType.MESH
bf16 = jnp.bfloat16
f32 = jnp.float32

ROUTE_SCALE = 2.5
N = 8
TOK = 64
TOP = 8
QUARTER = 896
HID = 1024
LATENT = 512
KV = 576
PAGE = 16
GROUPS = ((0, 1, 7), (3, 5, 4), (2, 6))
STEPS = ((0, 1, 7, 2), (6, 3, 5, 4))
CHUNKS = (
    (0, STEPS[0], 128),
    (0, STEPS[1], 128),
    (1, STEPS[0], 128),
    (1, STEPS[1], 128),
    (2, STEPS[0], 80),
    (2, STEPS[1], 80),
)
LAST_LANES = 640
COUNT = len(CHUNKS)
MOST = max(chunk[2] for chunk in CHUNKS)


def dot(a, b):
    return jnp.dot(a, b, preferred_element_type=f32)


def put(ref, group, slots, rows):
    if group < 2:
        for i, at in enumerate(slots):
            ref[at] = rows[16 * i : 16 * i + 16].astype(bf16)
        return

    def folded(r):
        parts = [rows[r : r + 1, 128 * k : 128 * k + 128] for k in range(7)]
        return jnp.concatenate(parts + [jnp.zeros((1, 128), f32)], axis=0)

    many = len(slots)
    for i, at in enumerate(slots):
        head = rows[8 * i : 8 * i + 8]
        rest = jnp.concatenate([head[:, 512:QUARTER], folded(8 * many + i)], axis=1)
        ref[at, :, 0:512] = jnp.concatenate([head[:, 0:512], rest], axis=0).astype(bf16)
        ref[at, :, 512:640] = jnp.concatenate([folded(9 * many + i), jnp.zeros((8, 128), f32)], axis=0).astype(bf16)


def take(ref, group, slots):
    if group < 2:
        return jnp.concatenate([ref[at] for at in slots], axis=0)

    def unfolded(part):
        return jnp.concatenate([part[k : k + 1] for k in range(7)], axis=1)

    heads, first, second = [], [], []
    for at in slots:
        head = ref[at, :, 0:512].astype(f32)
        heads.append(jnp.concatenate([head[0:8], head[8:16, 0:384]], axis=1))
        first.append(unfolded(head[8:16, 384:512]))
        second.append(unfolded(ref[at, :, 512:640].astype(f32)))
    return jnp.concatenate(heads + first + second, axis=0).astype(bf16)


def kernel(
    tok_hbm,
    ids_hbm,
    scores_hbm,
    up_hbm,
    down_hbm,
    lat_hbm,
    gain_hbm,
    owner_ref,
    freq_hbm,
    out_ref,
    kv_ref,
    tok_ref,
    ids_ref,
    scores_ref,
    gain_ref,
    freq_ref,
    up_ref,
    down_ref,
    lat_ref,
    tok_0,
    tok_1,
    tok_2,
    line_meta,
    code_0,
    code_1,
    code_2,
    wsel_0,
    wsel_1,
    wsel_2,
    disp_out_0,
    disp_out_1,
    disp_in_0,
    disp_in_1,
    back_out_0,
    back_out_1,
    back_in_0,
    back_in_1,
    disp_out_2,
    disp_in_2,
    back_out_2,
    back_in_2,
    chain_out,
    chain_in,
    part_ref,
    full_out,
    full_in,
    hid_ref,
    pick_ref,
    sum_0,
    sum_1,
    sum_2,
    line_out,
    line_in,
    lat_out,
    lat_own,
    lat_in,
    load_sem,
    tok_send,
    tok_recv,
    meta_send,
    meta_recv,
    disp_send,
    disp_recv,
    back_send,
    back_recv,
    chain_send,
    chain_recv,
    full_send,
    full_recv,
    hid_send,
    hid_recv,
    line_send,
    line_recv,
    lat_send,
    lat_recv,
):
    group_tok = (tok_0, tok_1, tok_2)
    code = (code_0, code_1, code_2)
    wsel = (wsel_0, wsel_1, wsel_2)
    disp_out = (disp_out_0, disp_out_1, disp_out_2)
    disp_in = (disp_in_0, disp_in_1, disp_in_2)
    back_out = (back_out_0, back_out_1, back_out_2)
    back_in = (back_in_0, back_in_1, back_in_2)
    sums = (sum_0, sum_1, sum_2)
    ep = lax.axis_index("ep")
    x = lax.axis_index("dec")
    core = lax.rem(ep, 2)
    chip = lax.div(ep, 2)
    z = lax.div(chip, N)
    y = lax.rem(chip, N)
    on_z = core == 0
    mine = jnp.where(on_z, z, y)
    cross = jnp.where(on_z, y, z)

    def wrap(v):
        return lax.rem(v + 2 * N, N)

    def line_dev(step):
        place = wrap(mine + step)
        zz = jnp.where(on_z, place, z)
        yy = jnp.where(on_z, y, place)
        return ((zz * N + yy) * 2 + core, x)

    def expert_dev(step, c):
        place = wrap(cross + step)
        zz = jnp.where(on_z, z, place)
        yy = jnp.where(on_z, place, y)
        return ((zz * N + yy) * 2 + c, x)

    def source_dev(c_src, step):
        if c_src == 0:
            return ((z * N + wrap(y - step)) * 2, x)
        return ((wrap(z - step) * N + y) * 2 + 1, x)

    def dec_dev(step):
        return (ep, lax.rem(x + step + 4, 4))

    sent = []

    def send(src, dst, s_sem, r_sem, dev):
        copy = pltpu.make_async_remote_copy(
            src_ref=src, dst_ref=dst, send_sem=s_sem, recv_sem=r_sem, device_id=dev, device_id_type=MESH
        )
        copy.start()
        sent.append(copy)

    def arrived(dst, sem):
        pltpu.make_async_copy(dst, dst, sem).wait()

    loads = [
        pltpu.make_async_copy(src, dst, load_sem.at[i])
        for i, (src, dst) in enumerate(
            (
                (ids_hbm, ids_ref),
                (scores_hbm, scores_ref),
                (tok_hbm, tok_ref),
                (lat_hbm, lat_ref),
                (gain_hbm, gain_ref),
                (freq_hbm, freq_ref),
                (up_hbm.at[0], up_ref),
                (down_hbm.at[0], down_ref),
            )
        )
    ]
    for load in loads:
        load.start()

    barrier = pltpu.get_barrier_semaphore()

    def greet(dev):
        pl.semaphore_signal(barrier, inc=1, device_id=dev, device_id_type=MESH)

    greet(((z * N + y) * 2 + 1 - core, x))
    for step in range(1, N):
        for c in range(2):
            greet(((z * N + wrap(y + step)) * 2 + c, x))
            greet(((wrap(z + step) * N + y) * 2 + c, x))
    for step in range(1, 4):
        greet(dec_dev(step))

    loads[0].wait()
    loads[1].wait()
    gate = jax.nn.sigmoid(scores_ref[...])
    weight = ROUTE_SCALE * gate / jnp.sum(gate, axis=0, keepdims=True)
    line_meta[0] = jnp.concatenate([ids_ref[...].astype(f32), weight], axis=1)
    for group in range(2):
        group_tok[group][3] = jnp.zeros((TOK, QUARTER), bf16)
    loads[2].wait()

    pl.semaphore_wait(barrier, 4 * (N - 1) + 4)

    def place_of(rel):
        group = [rel in rels for rels in GROUPS].index(True)
        return group_tok[group].at[GROUPS[group].index(rel)]

    blocks = []

    def spread(src, rel, step, rows):
        at = len(blocks)
        dst = place_of(rel).at[pl.ds(*rows)]
        blocks.append((rel, rows, at))
        send(src.at[pl.ds(*rows)], dst, tok_send.at[at], tok_recv.at[at], line_dev(step))

    def taken(rel, rows):
        at = [b[2] for b in blocks if b[0] == rel and b[1] == rows][0]
        arrived(place_of(rel).at[pl.ds(*rows)], tok_recv.at[at])

    whole, low_half, high_half = (0, TOK), (0, TOK // 2), (TOK // 2, TOK // 2)
    for step in range(1, N):
        send(line_meta.at[0], line_meta.at[step], meta_send.at[step - 1], meta_recv.at[step - 1], line_dev(step))
    spread(tok_ref, 1, 1, whole)
    spread(tok_ref, 7, -1, whole)
    spread(tok_ref, 2, 2, low_half)
    spread(tok_ref, 6, -2, high_half)
    spread(tok_ref, 2, 2, high_half)
    spread(tok_ref, 6, -2, low_half)
    tok_0[0] = tok_ref[...]

    lane = lax.broadcasted_iota(jnp.int32, (TOK, TOK), 1)
    row = lax.broadcasted_iota(jnp.int32, (TOK, TOK), 0)
    owner_of = jnp.zeros((TOK, TOK), jnp.int32)
    page = jnp.int32(0)
    for p in range(4):
        owner_of = jnp.where((lane >> 4) == p, owner_ref[p], owner_of)
        page = page + jnp.where(owner_ref[p] == x, p, 0)
    wanted = lax.rem((row >> 4) + x, 4)
    order = jnp.where((owner_of == wanted) & ((lane & 15) == (row & 15)), 1.0, 0.0).astype(bf16)
    ordered = dot(order, tok_ref[...]).astype(bf16)
    loads[3].wait()
    latent = lax.dot_general(ordered, lat_ref[...], (((1,), (1,)), ((), ())), preferred_element_type=f32)
    lat_own[...] = latent[0:PAGE]
    lat_out[...] = latent[PAGE:].astype(bf16).reshape(3, PAGE, KV)
    for step in range(1, 4):
        send(lat_out.at[step - 1], lat_in.at[step - 1], lat_send.at[step - 1], lat_recv.at[step - 1], dec_dev(step))

    low = lax.broadcasted_iota(jnp.int32, (TOP, 128), 1) < TOK
    before_r = lax.broadcasted_iota(jnp.int32, (128, 128), 0)
    before_c = lax.broadcasted_iota(jnp.int32, (128, 128), 1)
    before = jnp.where((before_r < before_c) & ((before_r >> 6) == (before_c >> 6)), 1.0, 0.0).astype(bf16)
    number = lax.broadcasted_iota(jnp.int32, (16, 128), 0)
    place = lax.rem(cross + (number >> 1), N)
    expert = jnp.where(on_z, 16 * mine + 2 * place, 16 * place + 2 * mine) + (number & 1)
    expert = expert.astype(f32)

    coded = []

    def codes(group):
        if group in coded:
            return
        coded.append(group)
        rels = GROUPS[group]
        for rel in rels:
            if rel:
                arrived(line_meta.at[rel], meta_recv.at[rel - 1])
        for pair in range((len(rels) + 1) // 2):
            even = line_meta[rels[2 * pair]]
            if 2 * pair + 1 < len(rels):
                odd = line_meta[rels[2 * pair + 1]]
                ids = jnp.where(low, even, pltpu.roll(odd, TOK, 1))
            else:
                odd = jnp.zeros_like(even)
                ids = jnp.where(low, even, -1.0)
            weights = jnp.where(low, pltpu.roll(even, TOK, 1), odd)
            hits = jnp.zeros((16, 128), f32)
            chosen = jnp.zeros((16, 128), f32)
            for k in range(TOP):
                match = ids[k : k + 1, :] == expert
                hits = jnp.where(match, 1.0, hits)
                chosen = jnp.where(match, weights[k : k + 1, :], chosen)
            rank = dot(hits.astype(bf16), before)
            code[group][:, 128 * pair : 128 * pair + 128] = jnp.where(hits > 0.5, rank, -1.0)
            wsel[group][:, 128 * pair : 128 * pair + 128] = chosen

    wide_row = lax.broadcasted_iota(jnp.int32, (16, 256), 0)
    wide_block = lax.broadcasted_iota(jnp.int32, (16, 256), 1) >> 6
    wide_slot = (wide_row * 11) >> 5
    wide_pattern = jnp.where(wide_block == wide_row - 3 * wide_slot, wide_slot, -2).astype(f32)
    slim_row = lax.broadcasted_iota(jnp.int32, (8, 128), 0)
    slim_block = lax.broadcasted_iota(jnp.int32, (8, 128), 1) >> 6
    slim_pattern = jnp.where(slim_block == (slim_row & 1), slim_row >> 1, -2).astype(f32)

    def picks(group, steps, weighted):
        codes(group)

        def match(at, many, pat):
            value = wsel[group][at : at + many, :] if weighted else 1.0
            return jnp.where(code[group][at : at + many, :] == pat, value, 0.0)

        slots = [2 * step + c for step in steps for c in range(2)]
        if group < 2:
            return jnp.concatenate([match(at, 1, wide_pattern) for at in slots], axis=0)
        heads = [match(at, 1, slim_pattern) for at in slots]
        lasts = [
            match(2 * step, 2, jnp.where(slim_block[0:2] == block, 4.0, -2.0)) for block in range(2) for step in steps
        ]
        return jnp.concatenate(heads + lasts, axis=0)

    def stage_disp(j):
        group, steps, _ = CHUNKS[j]
        tok = group_tok[group]
        rows = dot(picks(group, steps, False).astype(bf16), tok[...].reshape(tok.shape[0] * TOK, QUARTER))
        put(disp_out[group], group, [2 * step + c for step in steps for c in range(2)], rows)
        out, into = disp_out[group], disp_in[group]
        for step in steps:
            slot = N * core + step
            s_at, r_at = 16 * group, 16 * group + slot
            if step == 0:
                pltpu.make_async_copy(out.at[core], into.at[slot], disp_recv.at[r_at]).start()
                other = 1 - core
                send(out.at[other], into.at[slot], disp_send.at[s_at + other], disp_recv.at[r_at], expert_dev(0, other))
            else:
                for c in range(2):
                    at = 2 * step + c
                    send(out.at[at], into.at[slot], disp_send.at[s_at + at], disp_recv.at[r_at], expert_dev(step, c))

    def stage_pick(j):
        group, steps, many = CHUNKS[j]
        tokens = group_tok[group].shape[0] * TOK
        pick_ref[j, 0:tokens, 0:many] = picks(group, steps, True).T.astype(bf16)

    def stage_latent():
        for step in range(1, 4):
            arrived(lat_in.at[step - 1], lat_recv.at[step - 1])
        loads[4].wait()
        loads[5].wait()
        total = lat_own[...]
        for step in range(3):
            total = total + lat_in[step].astype(f32)
        comp = total[:, 0:LATENT]
        scale = lax.rsqrt(jnp.sum(comp * comp, axis=1, keepdims=True) * (1.0 / LATENT) + 1e-6)
        kv_ref[:, 0:LATENT] = (comp * scale * gain_ref[...]).astype(bf16)
        half = (KV - LATENT) // 2
        first, second = total[:, LATENT : LATENT + half], total[:, LATENT + half :]
        token = (ep * TOK + page * PAGE + lax.broadcasted_iota(jnp.int32, (PAGE, half), 0)).astype(f32)
        angle = token * freq_ref[...]
        cos, sin = jnp.cos(angle), jnp.sin(angle)
        kv_ref[:, LATENT:] = jnp.concatenate(
            [first * cos - second * sin, second * cos + first * sin], axis=1
        ).astype(bf16)

    loaded = []

    def quarter_of(step):
        return pl.ds(pl.multiple_of(lax.rem(x + step + 4, 4) * 256, 256), 256)

    def stage_up(j):
        group, steps, many = CHUNKS[j]
        slots = [N * c + step for step in steps for c in range(2)]
        for slot in slots:
            arrived(disp_in[group].at[slot], disp_recv.at[16 * group + slot])
        block = take(disp_in[group], group, slots)
        if 6 not in loaded:
            loads[6].wait()
            loaded.append(6)
        part = dot(block, up_ref[:, quarter_of(2)])
        for d in range(2):
            chain_out[j, d, 0:many] = part[:, 128 * d : 128 * d + 128].astype(bf16)
            at = 2 * j + d
            send(
                chain_out.at[j, d, pl.ds(0, many)],
                chain_in.at[j, d, pl.ds(0, many)],
                chain_send.at[at],
                chain_recv.at[at],
                dec_dev(1 if d == 0 else -1),
            )
        part_ref[j, 0, 0:many] = dot(block, up_ref[:, quarter_of(1)])
        part_ref[j, 1, 0:many] = dot(block, up_ref[:, quarter_of(-1)])
        part_ref[j, 2, 0:many] = dot(block, up_ref[:, quarter_of(0)])

    def stage_chain(j):
        many = CHUNKS[j][2]
        for d in range(2):
            at = 2 * j + d
            arrived(chain_in.at[j, d, pl.ds(0, many)], chain_recv.at[at])
            for half in range(2):
                value = part_ref[j, d, 0:many, 128 * half : 128 * half + 128]
                if half == d:
                    value = value + chain_in[j, d, 0:many].astype(f32)
                full_out[j, d, half, 0:many] = value.astype(bf16)
            send(
                full_out.at[j, d, :, pl.ds(0, many)],
                full_in.at[j, d, :, pl.ds(0, many)],
                full_send.at[at],
                full_recv.at[at],
                dec_dev(1 if d == 0 else -1),
            )

    def stage_hidden(j):
        many = CHUNKS[j][2]
        for d in range(2):
            arrived(full_in.at[j, d, :, pl.ds(0, many)], full_recv.at[2 * j + d])
        for half in range(2):
            pre = part_ref[j, 2, 0:many, 128 * half : 128 * half + 128]
            pre = pre + full_in[j, 0, half, 0:many].astype(f32) + full_in[j, 1, half, 0:many].astype(f32)
            hid_ref[j, 0, half, 0:many] = (pre / (1.0 + jnp.exp(-pre))).astype(bf16)
        for d in range(2):
            send(
                hid_ref.at[j, 0, :, pl.ds(0, many)],
                hid_ref.at[j, 1 + d, :, pl.ds(0, many)],
                hid_send.at[4 * j + d],
                hid_recv.at[4 * j + d],
                dec_dev(1 if d == 0 else -1),
            )

    def stage_pass(j):
        many = CHUNKS[j][2]
        for d in range(2):
            arrived(hid_ref.at[j, 1 + d, :, pl.ds(0, many)], hid_recv.at[4 * j + d])
            send(
                hid_ref.at[j, 1 + d, d, pl.ds(0, many)],
                hid_ref.at[j, 3, d, pl.ds(0, many)],
                hid_send.at[4 * j + 2 + d],
                hid_recv.at[4 * j + 2 + d],
                dec_dev(1 if d == 0 else -1),
            )

    def stage_down(j):
        group, steps, many = CHUNKS[j]
        if 7 not in loaded:
            loads[7].wait()
            loaded.append(7)
        total = None
        for place, step in ((0, 0), (1, -1), (2, 1), (3, 2)):
            if place == 3:
                for d in range(2):
                    arrived(hid_ref.at[j, 3, d, pl.ds(0, many)], hid_recv.at[4 * j + 2 + d])
            hidden = jnp.concatenate([hid_ref[j, place, 0, 0:many], hid_ref[j, place, 1, 0:many]], axis=1)
            term = dot(hidden, down_ref[quarter_of(step), :])
            total = term if total is None else total + term
        put(back_out[group], group, [N * c + step for step in steps for c in range(2)], total)
        out, into = back_out[group], back_in[group]
        for step in steps:
            slot = 2 * step + core
            s_at, r_at = 16 * group, 16 * group + slot
            if step == 0:
                own, other = N * core, N * (1 - core)
                pltpu.make_async_copy(out.at[own], into.at[slot], back_recv.at[r_at]).start()
                mate = ((z * N + y) * 2 + 1 - core, x)
                send(out.at[other], into.at[slot], back_send.at[s_at + other], back_recv.at[r_at], mate)
            else:
                for c in range(2):
                    at = N * c + step
                    send(out.at[at], into.at[slot], back_send.at[s_at + at], back_recv.at[r_at], source_dev(c, step))

    summed = [0, 0, 0]

    def stage_sum(j):
        group, steps, many = CHUNKS[j]
        slots = [2 * step + c for step in steps for c in range(2)]
        for slot in slots:
            arrived(back_in[group].at[slot], back_recv.at[16 * group + slot])
        block = take(back_in[group], group, slots)
        rels = GROUPS[group]
        total = dot(pick_ref[j, 0 : TOK * len(rels), 0:many], block)
        if summed[group]:
            total = total + sums[group][...]
        summed[group] += 1
        if summed[group] < len([c for c in CHUNKS if c[0] == group]):
            sums[group][...] = total
            return
        if group == 0:
            sums[0][0:TOK] = total[0:TOK]
        def give(rel, step, rows):
            at = rel - 1 if rel != 4 or rows == low_half else 7
            part = pl.ds(*rows)
            send(line_out.at[rel - 1, part], line_in.at[rel - 1, part], line_send.at[at], line_recv.at[at], line_dev(step))

        if group == 2:
            for rel, part in ((3, whole), (5, whole), (4, low_half), (4, high_half)):
                at = rel - 1 if rel != 4 or part == low_half else 7
                arrived(line_in.at[rel - 1, pl.ds(*part)], line_recv.at[at])
            middle = line_in[3].astype(f32)
            total = total + jnp.concatenate(
                [
                    line_in[2, 0:32].astype(f32) + middle[0:32],
                    line_in[2, 32:64].astype(f32),
                    line_in[4, 0:32].astype(f32),
                    line_in[4, 32:64].astype(f32) + middle[32:64],
                ],
                axis=0,
            )
        for i, rel in enumerate(rels):
            if rel:
                line_out[rel - 1] = total[TOK * i : TOK * i + TOK].astype(bf16)
        if group == 0:
            give(1, -1, whole)
            give(7, 1, whole)
        elif group == 1:
            give(4, -2, low_half)
            give(4, 2, high_half)
            give(3, -1, whole)
            give(5, 1, whole)
        else:
            give(2, -2, whole)
            give(6, 2, whole)

    def wait_near():
        for rel in GROUPS[0][1:]:
            taken(rel, whole)

    def pass_far():
        taken(2, low_half)
        spread(place_of(2), 4, 2, low_half)
        taken(6, high_half)
        spread(place_of(6), 4, -2, high_half)
        taken(2, high_half)
        spread(place_of(2), 3, 1, whole)
        taken(6, low_half)
        spread(place_of(6), 5, -1, whole)

    def wait_far():
        for rel, rows in ((3, whole), (5, whole), (4, low_half), (4, high_half)):
            taken(rel, rows)

    wait_near()
    stage_disp(0)
    pass_far()
    stage_pick(5)
    stage_disp(5)
    stage_pick(0)
    stage_up(0)
    stage_disp(4)
    stage_chain(0)
    wait_far()
    stage_disp(3)
    stage_latent()
    stage_disp(2)
    stage_up(5)
    stage_up(4)
    stage_hidden(0)
    stage_disp(1)
    stage_chain(5)
    stage_chain(4)
    stage_up(3)
    stage_pass(0)
    stage_hidden(5)
    stage_hidden(4)
    stage_chain(3)
    stage_pass(5)
    stage_up(2)
    stage_pass(4)
    stage_up(1)
    stage_pick(2)
    stage_hidden(3)
    stage_down(5)
    stage_chain(2)
    stage_chain(1)
    stage_pick(1)
    stage_down(4)
    stage_pick(3)
    stage_pass(3)
    stage_down(0)
    stage_hidden(2)
    stage_pick(4)
    stage_hidden(1)
    stage_pass(2)
    stage_down(3)
    stage_pass(1)
    stage_down(2)
    stage_down(1)
    stage_sum(2)
    stage_sum(3)
    stage_sum(0)
    stage_sum(1)
    stage_sum(4)
    stage_sum(5)

    total = sum_0[0:TOK]
    for rel in (1, 7, 2, 6):
        arrived(line_in.at[rel - 1], line_recv.at[rel - 1])
        total = total + line_in[rel - 1].astype(f32)
    out_ref[...] = total.astype(bf16)

    for copy in sent:
        copy.wait_send()


def on_device(tokens, expert_ids, route_scores, up_weight, down_weight, latent_weight, latent_norm_gain, page_owner):
    half = (KV - LATENT) // 2
    freq = np.power(10000.0, -np.arange(half, dtype=np.float64) / half).astype(np.float32)
    vmem = pl.BlockSpec(memory_space=pltpu.VMEM)
    hbm = pl.BlockSpec(memory_space=pl.ANY)
    smem = pl.BlockSpec(memory_space=pltpu.SMEM)
    dma = pltpu.SemaphoreType.DMA
    return pl.pallas_call(
        kernel,
        out_shape=(
            jax.ShapeDtypeStruct((TOK, QUARTER), bf16),
            jax.ShapeDtypeStruct((PAGE, KV), bf16),
        ),
        in_specs=[hbm, hbm, hbm, hbm, hbm, hbm, hbm, smem, hbm],
        out_specs=(vmem, vmem),
        scratch_shapes=[
            pltpu.VMEM((TOK, QUARTER), bf16),
            pltpu.VMEM((TOP, TOK), jnp.int32),
            pltpu.VMEM((TOP, TOK), f32),
            pltpu.VMEM((1, LATENT), f32),
            pltpu.VMEM((1, half), f32),
            pltpu.VMEM((QUARTER, HID), bf16),
            pltpu.VMEM((HID, QUARTER), bf16),
            pltpu.VMEM((KV, QUARTER), bf16),
            pltpu.VMEM((4, TOK, QUARTER), bf16),
            pltpu.VMEM((4, TOK, QUARTER), bf16),
            pltpu.VMEM((2, TOK, QUARTER), bf16),
            pltpu.VMEM((N, TOP, 128), f32),
        ]
        + [pltpu.VMEM((16, lanes), f32) for lanes in (256, 256, 128)] * 2
        + [pltpu.VMEM((16, 16, QUARTER), bf16)] * 8
        + [pltpu.VMEM((16, 16, LAST_LANES), bf16)] * 4
        + [
            pltpu.VMEM((COUNT, 2, MOST, 128), bf16),
            pltpu.VMEM((COUNT, 2, MOST, 128), bf16),
            pltpu.VMEM((COUNT, 3, MOST, 256), f32),
            pltpu.VMEM((COUNT, 2, 2, MOST, 128), bf16),
            pltpu.VMEM((COUNT, 2, 2, MOST, 128), bf16),
            pltpu.VMEM((COUNT, 4, 2, MOST, 128), bf16),
            pltpu.VMEM((COUNT, 256, MOST), bf16),
            pltpu.VMEM((3 * TOK, QUARTER), f32),
            pltpu.VMEM((3 * TOK, QUARTER), f32),
            pltpu.VMEM((2 * TOK, QUARTER), f32),
            pltpu.VMEM((7, TOK, QUARTER), bf16),
            pltpu.VMEM((7, TOK, QUARTER), bf16),
            pltpu.VMEM((3, PAGE, KV), bf16),
            pltpu.VMEM((PAGE, KV), f32),
            pltpu.VMEM((3, PAGE, KV), bf16),
        ]
        + [
            dma((count,))
            for count in (8, 10, 10, 7, 7, 48, 48, 48, 48)
            + (2 * COUNT,) * 4
            + (4 * COUNT, 4 * COUNT, 8, 8, 3, 3)
        ],
        compiler_params=pltpu.CompilerParams(
            collective_id=0, has_side_effects=True, vmem_limit_bytes=60 * 1024 * 1024
        ),
    )(
        tokens,
        expert_ids.T,
        route_scores.T,
        up_weight,
        down_weight,
        latent_weight.T,
        latent_norm_gain.reshape(1, LATENT),
        page_owner,
        jnp.asarray(freq).reshape(1, half),
    )


def solution(mesh):
    placed = (
        P("ep", "dec"),
        P("ep", None),
        P("ep", None),
        P("ep", "dec", None),
        P("ep", None, "dec"),
        P("dec", None),
        P(),
        P("ep"),
    )
    return jax.shard_map(
        on_device,
        mesh=mesh,
        in_specs=placed,
        out_specs=(P("ep", "dec"), P(("ep", "dec"), None)),
        check_vma=False,
    )
```

```python
import functools

import jax
import jax.numpy as jnp
import numpy as np
from jax import lax
from jax.experimental import pallas as pl
from jax.experimental.pallas import tpu as pltpu
from jax.sharding import PartitionSpec as P

MESH = pl.DeviceIdType.MESH
bf16 = jnp.bfloat16
f32 = jnp.float32

ROUTE_SCALE = 2.5
N = 8
TOK = 64
TOP = 8
QUARTER = 896
HID = 1024
LATENT = 512
KV = 576
PAGE = 16
GROUPS = ((0, 1, 7), (3, 5, 4), (2, 6))
STEPS = ((0, 1, 7, 2), (6, 3, 5, 4))
CHUNKS = (
    (0, STEPS[0], 128),
    (0, STEPS[1], 128),
    (1, STEPS[0], 128),
    (1, STEPS[1], 128),
    (2, STEPS[0], 80),
    (2, STEPS[1], 80),
)
LAST_LANES = 640
COUNT = len(CHUNKS)
MOST = max(chunk[2] for chunk in CHUNKS)


def dot(a, b):
    return jnp.dot(a, b, preferred_element_type=f32)


def put(ref, group, slots, rows):
    if group < 2:
        for i, at in enumerate(slots):
            ref[at] = rows[16 * i : 16 * i + 16].astype(bf16)
        return

    def folded(r):
        parts = [rows[r : r + 1, 128 * k : 128 * k + 128] for k in range(7)]
        return jnp.concatenate(parts + [jnp.zeros((1, 128), f32)], axis=0)

    many = len(slots)
    for i, at in enumerate(slots):
        head = rows[8 * i : 8 * i + 8]
        rest = jnp.concatenate([head[:, 512:QUARTER], folded(8 * many + i)], axis=1)
        ref[at, :, 0:512] = jnp.concatenate([head[:, 0:512], rest], axis=0).astype(bf16)
        ref[at, :, 512:640] = jnp.concatenate([folded(9 * many + i), jnp.zeros((8, 128), f32)], axis=0).astype(bf16)


def take(ref, group, slots):
    if group < 2:
        return jnp.concatenate([ref[at] for at in slots], axis=0)

    def unfolded(part):
        return jnp.concatenate([part[k : k + 1] for k in range(7)], axis=1)

    heads, first, second = [], [], []
    for at in slots:
        head = ref[at, :, 0:512].astype(f32)
        heads.append(jnp.concatenate([head[0:8], head[8:16, 0:384]], axis=1))
        first.append(unfolded(head[8:16, 384:512]))
        second.append(unfolded(ref[at, :, 512:640].astype(f32)))
    return jnp.concatenate(heads + first + second, axis=0).astype(bf16)


def kernel(
    tok_hbm,
    ids_hbm,
    scores_hbm,
    up_hbm,
    down_hbm,
    lat_hbm,
    gain_hbm,
    owner_ref,
    freq_hbm,
    out_ref,
    kv_ref,
    tok_ref,
    ids_ref,
    scores_ref,
    gain_ref,
    freq_ref,
    up_ref,
    down_ref,
    lat_ref,
    tok_0,
    tok_1,
    tok_2,
    line_meta,
    code_0,
    code_1,
    code_2,
    wsel_0,
    wsel_1,
    wsel_2,
    disp_out_0,
    disp_out_1,
    disp_in_0,
    disp_in_1,
    back_out_0,
    back_out_1,
    back_in_0,
    back_in_1,
    disp_out_2,
    disp_in_2,
    back_out_2,
    back_in_2,
    chain_out,
    chain_in,
    part_ref,
    full_out,
    full_in,
    hid_ref,
    pick_ref,
    sum_0,
    sum_1,
    sum_2,
    line_out,
    line_in,
    lat_out,
    lat_own,
    lat_in,
    load_sem,
    tok_send,
    tok_recv,
    meta_send,
    meta_recv,
    disp_send,
    disp_recv,
    back_send,
    back_recv,
    chain_send,
    chain_recv,
    full_send,
    full_recv,
    hid_send,
    hid_recv,
    line_send,
    line_recv,
    lat_send,
    lat_recv,
):
    group_tok = (tok_0, tok_1, tok_2)
    code = (code_0, code_1, code_2)
    wsel = (wsel_0, wsel_1, wsel_2)
    disp_out = (disp_out_0, disp_out_1, disp_out_2)
    disp_in = (disp_in_0, disp_in_1, disp_in_2)
    back_out = (back_out_0, back_out_1, back_out_2)
    back_in = (back_in_0, back_in_1, back_in_2)
    sums = (sum_0, sum_1, sum_2)
    ep = lax.axis_index("ep")
    x = lax.axis_index("dec")
    core = lax.rem(ep, 2)
    chip = lax.div(ep, 2)
    z = lax.div(chip, N)
    y = lax.rem(chip, N)
    on_z = core == 0
    mine = jnp.where(on_z, z, y)
    cross = jnp.where(on_z, y, z)

    def wrap(v):
        return lax.rem(v + 2 * N, N)

    def line_dev(step):
        place = wrap(mine + step)
        zz = jnp.where(on_z, place, z)
        yy = jnp.where(on_z, y, place)
        return ((zz * N + yy) * 2 + core, x)

    def expert_dev(step, c):
        place = wrap(cross + step)
        zz = jnp.where(on_z, z, place)
        yy = jnp.where(on_z, place, y)
        return ((zz * N + yy) * 2 + c, x)

    def source_dev(c_src, step):
        if c_src == 0:
            return ((z * N + wrap(y - step)) * 2, x)
        return ((wrap(z - step) * N + y) * 2 + 1, x)

    def dec_dev(step):
        return (ep, lax.rem(x + step + 4, 4))

    sent = []

    def send(src, dst, s_sem, r_sem, dev):
        copy = pltpu.make_async_remote_copy(
            src_ref=src, dst_ref=dst, send_sem=s_sem, recv_sem=r_sem, device_id=dev, device_id_type=MESH
        )
        copy.start()
        sent.append(copy)

    def arrived(dst, sem):
        pltpu.make_async_copy(dst, dst, sem).wait()

    barrier = pltpu.get_barrier_semaphore()

    def greet(dev):
        pl.semaphore_signal(barrier, inc=1, device_id=dev, device_id_type=MESH)

    greet(((z * N + y) * 2 + 1 - core, x))
    for step in range(1, N):
        for c in range(2):
            greet(((z * N + wrap(y + step)) * 2 + c, x))
            greet(((wrap(z + step) * N + y) * 2 + c, x))
    for step in range(1, 4):
        greet(dec_dev(step))

    loads = [
        pltpu.make_async_copy(src, dst, load_sem.at[i])
        for i, (src, dst) in enumerate(
            (
                (ids_hbm, ids_ref),
                (scores_hbm, scores_ref),
                (tok_hbm, tok_ref),
                (lat_hbm, lat_ref),
                (gain_hbm, gain_ref),
                (freq_hbm, freq_ref),
                (up_hbm.at[0], up_ref),
                (down_hbm.at[0], down_ref),
            )
        )
    ]
    for load in loads:
        load.start()

    loads[0].wait()
    loads[1].wait()
    gate = jax.nn.sigmoid(scores_ref[...])
    weight = ROUTE_SCALE * gate / jnp.sum(gate, axis=0, keepdims=True)
    line_meta[0] = jnp.concatenate([ids_ref[...].astype(f32), weight], axis=1)
    for group in range(2):
        group_tok[group][3] = jnp.zeros((TOK, QUARTER), bf16)
    loads[2].wait()

    pl.semaphore_wait(barrier, 4 * (N - 1) + 4)

    def place_of(rel):
        group = [rel in rels for rels in GROUPS].index(True)
        return group_tok[group].at[GROUPS[group].index(rel)]

    blocks = []

    def spread(src, rel, step, rows):
        at = len(blocks)
        dst = place_of(rel).at[pl.ds(*rows)]
        blocks.append((rel, rows, at))
        send(src.at[pl.ds(*rows)], dst, tok_send.at[at], tok_recv.at[at], line_dev(step))

    def taken(rel, rows):
        at = [b[2] for b in blocks if b[0] == rel and b[1] == rows][0]
        arrived(place_of(rel).at[pl.ds(*rows)], tok_recv.at[at])

    whole, low_half, high_half = (0, TOK), (0, TOK // 2), (TOK // 2, TOK // 2)
    for step in range(1, N):
        send(line_meta.at[0], line_meta.at[step], meta_send.at[step - 1], meta_recv.at[step - 1], line_dev(step))
    spread(tok_ref, 1, 1, whole)
    spread(tok_ref, 7, -1, whole)
    spread(tok_ref, 2, 2, low_half)
    spread(tok_ref, 6, -2, high_half)
    spread(tok_ref, 2, 2, high_half)
    spread(tok_ref, 6, -2, low_half)
    tok_0[0] = tok_ref[...]

    lane = lax.broadcasted_iota(jnp.int32, (TOK, TOK), 1)
    row = lax.broadcasted_iota(jnp.int32, (TOK, TOK), 0)
    owner_of = jnp.zeros((TOK, TOK), jnp.int32)
    page = jnp.int32(0)
    for p in range(4):
        owner_of = jnp.where((lane >> 4) == p, owner_ref[p], owner_of)
        page = page + jnp.where(owner_ref[p] == x, p, 0)
    wanted = lax.rem((row >> 4) + x, 4)
    order = jnp.where((owner_of == wanted) & ((lane & 15) == (row & 15)), 1.0, 0.0).astype(bf16)
    ordered = dot(order, tok_ref[...]).astype(bf16)
    loads[3].wait()
    latent = lax.dot_general(ordered, lat_ref[...], (((1,), (1,)), ((), ())), preferred_element_type=f32)
    lat_own[...] = latent[0:PAGE]
    lat_out[...] = latent[PAGE:].astype(bf16).reshape(3, PAGE, KV)
    for step in range(1, 4):
        send(lat_out.at[step - 1], lat_in.at[step - 1], lat_send.at[step - 1], lat_recv.at[step - 1], dec_dev(step))

    low = lax.broadcasted_iota(jnp.int32, (TOP, 128), 1) < TOK
    before_r = lax.broadcasted_iota(jnp.int32, (128, 128), 0)
    before_c = lax.broadcasted_iota(jnp.int32, (128, 128), 1)
    before = jnp.where((before_r < before_c) & ((before_r >> 6) == (before_c >> 6)), 1.0, 0.0).astype(bf16)
    number = lax.broadcasted_iota(jnp.int32, (16, 128), 0)
    place = lax.rem(cross + (number >> 1), N)
    expert = jnp.where(on_z, 16 * mine + 2 * place, 16 * place + 2 * mine) + (number & 1)
    expert = expert.astype(f32)

    coded = []

    def codes(group):
        if group in coded:
            return
        coded.append(group)
        rels = GROUPS[group]
        for rel in rels:
            if rel:
                arrived(line_meta.at[rel], meta_recv.at[rel - 1])
        for pair in range((len(rels) + 1) // 2):
            even = line_meta[rels[2 * pair]]
            if 2 * pair + 1 < len(rels):
                odd = line_meta[rels[2 * pair + 1]]
                ids = jnp.where(low, even, pltpu.roll(odd, TOK, 1))
            else:
                odd = jnp.zeros_like(even)
                ids = jnp.where(low, even, -1.0)
            weights = jnp.where(low, pltpu.roll(even, TOK, 1), odd)
            hits = jnp.zeros((16, 128), f32)
            chosen = jnp.zeros((16, 128), f32)
            for k in range(TOP):
                match = ids[k : k + 1, :] == expert
                hits = jnp.where(match, 1.0, hits)
                chosen = jnp.where(match, weights[k : k + 1, :], chosen)
            rank = dot(hits.astype(bf16), before)
            code[group][:, 128 * pair : 128 * pair + 128] = jnp.where(hits > 0.5, rank, -1.0)
            wsel[group][:, 128 * pair : 128 * pair + 128] = chosen

    wide_row = lax.broadcasted_iota(jnp.int32, (16, 256), 0)
    wide_block = lax.broadcasted_iota(jnp.int32, (16, 256), 1) >> 6
    wide_slot = (wide_row * 11) >> 5
    wide_pattern = jnp.where(wide_block == wide_row - 3 * wide_slot, wide_slot, -2).astype(f32)
    slim_row = lax.broadcasted_iota(jnp.int32, (8, 128), 0)
    slim_block = lax.broadcasted_iota(jnp.int32, (8, 128), 1) >> 6
    slim_pattern = jnp.where(slim_block == (slim_row & 1), slim_row >> 1, -2).astype(f32)

    def picks(group, steps, weighted):
        codes(group)

        def match(at, many, pat):
            value = wsel[group][at : at + many, :] if weighted else 1.0
            return jnp.where(code[group][at : at + many, :] == pat, value, 0.0)

        slots = [2 * step + c for step in steps for c in range(2)]
        if group < 2:
            return jnp.concatenate([match(at, 1, wide_pattern) for at in slots], axis=0)
        heads = [match(at, 1, slim_pattern) for at in slots]
        lasts = [
            match(2 * step, 2, jnp.where(slim_block[0:2] == block, 4.0, -2.0)) for block in range(2) for step in steps
        ]
        return jnp.concatenate(heads + lasts, axis=0)

    def stage_disp(j):
        group, steps, _ = CHUNKS[j]
        tok = group_tok[group]
        rows = dot(picks(group, steps, False).astype(bf16), tok[...].reshape(tok.shape[0] * TOK, QUARTER))
        put(disp_out[group], group, [2 * step + c for step in steps for c in range(2)], rows)
        out, into = disp_out[group], disp_in[group]
        for step in steps:
            slot = N * core + step
            s_at, r_at = 16 * group, 16 * group + slot
            if step == 0:
                pltpu.make_async_copy(out.at[core], into.at[slot], disp_recv.at[r_at]).start()
                other = 1 - core
                send(out.at[other], into.at[slot], disp_send.at[s_at + other], disp_recv.at[r_at], expert_dev(0, other))
            else:
                for c in range(2):
                    at = 2 * step + c
                    send(out.at[at], into.at[slot], disp_send.at[s_at + at], disp_recv.at[r_at], expert_dev(step, c))

    def stage_pick(j):
        group, steps, many = CHUNKS[j]
        tokens = group_tok[group].shape[0] * TOK
        pick_ref[j, 0:tokens, 0:many] = picks(group, steps, True).T.astype(bf16)

    def stage_latent():
        for step in range(1, 4):
            arrived(lat_in.at[step - 1], lat_recv.at[step - 1])
        loads[4].wait()
        loads[5].wait()
        total = lat_own[...]
        for step in range(3):
            total = total + lat_in[step].astype(f32)
        comp = total[:, 0:LATENT]
        scale = lax.rsqrt(jnp.sum(comp * comp, axis=1, keepdims=True) * (1.0 / LATENT) + 1e-6)
        kv_ref[:, 0:LATENT] = (comp * scale * gain_ref[...]).astype(bf16)
        half = (KV - LATENT) // 2
        first, second = total[:, LATENT : LATENT + half], total[:, LATENT + half :]
        token = (ep * TOK + page * PAGE + lax.broadcasted_iota(jnp.int32, (PAGE, half), 0)).astype(f32)
        angle = token * freq_ref[...]
        cos, sin = jnp.cos(angle), jnp.sin(angle)
        kv_ref[:, LATENT:] = jnp.concatenate(
            [first * cos - second * sin, second * cos + first * sin], axis=1
        ).astype(bf16)

    loaded = []

    def quarter_of(step):
        return pl.ds(pl.multiple_of(lax.rem(x + step + 4, 4) * 256, 256), 256)

    def stage_up(j):
        group, steps, many = CHUNKS[j]
        slots = [N * c + step for step in steps for c in range(2)]
        for slot in slots:
            arrived(disp_in[group].at[slot], disp_recv.at[16 * group + slot])
        block = take(disp_in[group], group, slots)
        if 6 not in loaded:
            loads[6].wait()
            loaded.append(6)
        part = dot(block, up_ref[:, quarter_of(2)])
        for d in range(2):
            chain_out[j, d, 0:many] = part[:, 128 * d : 128 * d + 128].astype(bf16)
            at = 2 * j + d
            send(
                chain_out.at[j, d, pl.ds(0, many)],
                chain_in.at[j, d, pl.ds(0, many)],
                chain_send.at[at],
                chain_recv.at[at],
                dec_dev(1 if d == 0 else -1),
            )
        part_ref[j, 0, 0:many] = dot(block, up_ref[:, quarter_of(1)])
        part_ref[j, 1, 0:many] = dot(block, up_ref[:, quarter_of(-1)])
        part_ref[j, 2, 0:many] = dot(block, up_ref[:, quarter_of(0)])

    def stage_chain(j):
        many = CHUNKS[j][2]
        for d in range(2):
            at = 2 * j + d
            arrived(chain_in.at[j, d, pl.ds(0, many)], chain_recv.at[at])
            for half in range(2):
                value = part_ref[j, d, 0:many, 128 * half : 128 * half + 128]
                if half == d:
                    value = value + chain_in[j, d, 0:many].astype(f32)
                full_out[j, d, half, 0:many] = value.astype(bf16)
            send(
                full_out.at[j, d, :, pl.ds(0, many)],
                full_in.at[j, d, :, pl.ds(0, many)],
                full_send.at[at],
                full_recv.at[at],
                dec_dev(1 if d == 0 else -1),
            )

    def stage_hidden(j):
        many = CHUNKS[j][2]
        for d in range(2):
            arrived(full_in.at[j, d, :, pl.ds(0, many)], full_recv.at[2 * j + d])
        for half in range(2):
            pre = part_ref[j, 2, 0:many, 128 * half : 128 * half + 128]
            pre = pre + full_in[j, 0, half, 0:many].astype(f32) + full_in[j, 1, half, 0:many].astype(f32)
            hid_ref[j, 0, half, 0:many] = (pre / (1.0 + jnp.exp(-pre))).astype(bf16)
        for d in range(2):
            send(
                hid_ref.at[j, 0, :, pl.ds(0, many)],
                hid_ref.at[j, 1 + d, :, pl.ds(0, many)],
                hid_send.at[4 * j + d],
                hid_recv.at[4 * j + d],
                dec_dev(1 if d == 0 else -1),
            )

    def stage_pass(j):
        many = CHUNKS[j][2]
        for d in range(2):
            arrived(hid_ref.at[j, 1 + d, :, pl.ds(0, many)], hid_recv.at[4 * j + d])
            send(
                hid_ref.at[j, 1 + d, d, pl.ds(0, many)],
                hid_ref.at[j, 3, d, pl.ds(0, many)],
                hid_send.at[4 * j + 2 + d],
                hid_recv.at[4 * j + 2 + d],
                dec_dev(1 if d == 0 else -1),
            )

    def stage_down(j):
        group, steps, many = CHUNKS[j]
        if 7 not in loaded:
            loads[7].wait()
            loaded.append(7)
        total = None
        for place, step in ((0, 0), (1, -1), (2, 1), (3, 2)):
            if place == 3:
                for d in range(2):
                    arrived(hid_ref.at[j, 3, d, pl.ds(0, many)], hid_recv.at[4 * j + 2 + d])
            hidden = jnp.concatenate([hid_ref[j, place, 0, 0:many], hid_ref[j, place, 1, 0:many]], axis=1)
            term = dot(hidden, down_ref[quarter_of(step), :])
            total = term if total is None else total + term
        put(back_out[group], group, [N * c + step for step in steps for c in range(2)], total)
        out, into = back_out[group], back_in[group]
        for step in steps:
            slot = 2 * step + core
            s_at, r_at = 16 * group, 16 * group + slot
            if step == 0:
                own, other = N * core, N * (1 - core)
                pltpu.make_async_copy(out.at[own], into.at[slot], back_recv.at[r_at]).start()
                mate = ((z * N + y) * 2 + 1 - core, x)
                send(out.at[other], into.at[slot], back_send.at[s_at + other], back_recv.at[r_at], mate)
            else:
                for c in range(2):
                    at = N * c + step
                    send(out.at[at], into.at[slot], back_send.at[s_at + at], back_recv.at[r_at], source_dev(c, step))

    summed = [0, 0, 0]

    def stage_sum(j):
        group, steps, many = CHUNKS[j]
        slots = [2 * step + c for step in steps for c in range(2)]
        for slot in slots:
            arrived(back_in[group].at[slot], back_recv.at[16 * group + slot])
        block = take(back_in[group], group, slots)
        rels = GROUPS[group]
        total = dot(pick_ref[j, 0 : TOK * len(rels), 0:many], block)
        if summed[group]:
            total = total + sums[group][...]
        summed[group] += 1
        if summed[group] < len([c for c in CHUNKS if c[0] == group]):
            sums[group][...] = total
            return
        if group == 0:
            sums[0][0:TOK] = total[0:TOK]
        def give(rel, step, rows):
            at = rel - 1 if rel != 4 or rows == low_half else 7
            part = pl.ds(*rows)
            send(line_out.at[rel - 1, part], line_in.at[rel - 1, part], line_send.at[at], line_recv.at[at], line_dev(step))

        if group == 2:
            for rel, part in ((3, whole), (5, whole), (4, low_half), (4, high_half)):
                at = rel - 1 if rel != 4 or part == low_half else 7
                arrived(line_in.at[rel - 1, pl.ds(*part)], line_recv.at[at])
            middle = line_in[3].astype(f32)
            total = total + jnp.concatenate(
                [
                    line_in[2, 0:32].astype(f32) + middle[0:32],
                    line_in[2, 32:64].astype(f32),
                    line_in[4, 0:32].astype(f32),
                    line_in[4, 32:64].astype(f32) + middle[32:64],
                ],
                axis=0,
            )
        for i, rel in enumerate(rels):
            if rel:
                line_out[rel - 1] = total[TOK * i : TOK * i + TOK].astype(bf16)
        if group == 0:
            give(1, -1, whole)
            give(7, 1, whole)
        elif group == 1:
            give(4, -2, low_half)
            give(4, 2, high_half)
            give(3, -1, whole)
            give(5, 1, whole)
        else:
            give(2, -2, whole)
            give(6, 2, whole)

    def wait_near():
        for rel in GROUPS[0][1:]:
            taken(rel, whole)

    def pass_far():
        taken(2, low_half)
        spread(place_of(2), 4, 2, low_half)
        taken(6, high_half)
        spread(place_of(6), 4, -2, high_half)
        taken(2, high_half)
        spread(place_of(2), 3, 1, whole)
        taken(6, low_half)
        spread(place_of(6), 5, -1, whole)

    def wait_far():
        for rel, rows in ((3, whole), (5, whole), (4, low_half), (4, high_half)):
            taken(rel, rows)

    wait_near()
    stage_disp(0)
    pass_far()
    stage_pick(5)
    stage_disp(5)
    stage_pick(0)
    stage_up(0)
    stage_disp(4)
    stage_chain(0)
    stage_latent()
    wait_far()
    stage_disp(3)
    stage_disp(2)
    stage_up(5)
    stage_up(4)
    stage_hidden(0)
    stage_disp(1)
    stage_chain(5)
    stage_chain(4)
    stage_up(3)
    stage_pass(0)
    stage_hidden(5)
    stage_hidden(4)
    stage_chain(3)
    stage_pass(5)
    stage_up(2)
    stage_pass(4)
    stage_up(1)
    stage_pick(2)
    stage_hidden(3)
    stage_down(5)
    stage_chain(2)
    stage_chain(1)
    stage_pick(1)
    stage_down(4)
    stage_pick(3)
    stage_pass(3)
    stage_down(0)
    stage_hidden(2)
    stage_pick(4)
    stage_hidden(1)
    stage_down(3)
    stage_pass(2)
    stage_pass(1)
    stage_down(2)
    stage_down(1)
    stage_sum(2)
    stage_sum(3)
    stage_sum(0)
    stage_sum(1)
    stage_sum(4)
    stage_sum(5)

    for copy in sent[:-8]:
        copy.wait_send()
    total = sum_0[0:TOK]
    for rel in (1, 7, 2, 6):
        arrived(line_in.at[rel - 1], line_recv.at[rel - 1])
        total = total + line_in[rel - 1].astype(f32)
    out_ref[...] = total.astype(bf16)

    for copy in sent[-8:]:
        copy.wait_send()


def on_device(tokens, expert_ids, route_scores, up_weight, down_weight, latent_weight, latent_norm_gain, page_owner):
    half = (KV - LATENT) // 2
    freq = np.power(10000.0, -np.arange(half, dtype=np.float64) / half).astype(np.float32)
    vmem = pl.BlockSpec(memory_space=pltpu.VMEM)
    hbm = pl.BlockSpec(memory_space=pl.ANY)
    smem = pl.BlockSpec(memory_space=pltpu.SMEM)
    dma = pltpu.SemaphoreType.DMA
    return pl.pallas_call(
        kernel,
        out_shape=(
            jax.ShapeDtypeStruct((TOK, QUARTER), bf16),
            jax.ShapeDtypeStruct((PAGE, KV), bf16),
        ),
        in_specs=[hbm, hbm, hbm, hbm, hbm, hbm, hbm, smem, hbm],
        out_specs=(vmem, vmem),
        scratch_shapes=[
            pltpu.VMEM((TOK, QUARTER), bf16),
            pltpu.VMEM((TOP, TOK), jnp.int32),
            pltpu.VMEM((TOP, TOK), f32),
            pltpu.VMEM((1, LATENT), f32),
            pltpu.VMEM((1, half), f32),
            pltpu.VMEM((QUARTER, HID), bf16),
            pltpu.VMEM((HID, QUARTER), bf16),
            pltpu.VMEM((KV, QUARTER), bf16),
            pltpu.VMEM((4, TOK, QUARTER), bf16),
            pltpu.VMEM((4, TOK, QUARTER), bf16),
            pltpu.VMEM((2, TOK, QUARTER), bf16),
            pltpu.VMEM((N, TOP, 128), f32),
        ]
        + [pltpu.VMEM((16, lanes), f32) for lanes in (256, 256, 128)] * 2
        + [pltpu.VMEM((16, 16, QUARTER), bf16)] * 8
        + [pltpu.VMEM((16, 16, LAST_LANES), bf16)] * 4
        + [
            pltpu.VMEM((COUNT, 2, MOST, 128), bf16),
            pltpu.VMEM((COUNT, 2, MOST, 128), bf16),
            pltpu.VMEM((COUNT, 3, MOST, 256), f32),
            pltpu.VMEM((COUNT, 2, 2, MOST, 128), bf16),
            pltpu.VMEM((COUNT, 2, 2, MOST, 128), bf16),
            pltpu.VMEM((COUNT, 4, 2, MOST, 128), bf16),
            pltpu.VMEM((COUNT, 256, MOST), bf16),
            pltpu.VMEM((3 * TOK, QUARTER), f32),
            pltpu.VMEM((3 * TOK, QUARTER), f32),
            pltpu.VMEM((2 * TOK, QUARTER), f32),
            pltpu.VMEM((7, TOK, QUARTER), bf16),
            pltpu.VMEM((7, TOK, QUARTER), bf16),
            pltpu.VMEM((3, PAGE, KV), bf16),
            pltpu.VMEM((PAGE, KV), f32),
            pltpu.VMEM((3, PAGE, KV), bf16),
        ]
        + [
            dma((count,))
            for count in (8, 10, 10, 7, 7, 48, 48, 48, 48)
            + (2 * COUNT,) * 4
            + (4 * COUNT, 4 * COUNT, 8, 8, 3, 3)
        ],
        compiler_params=pltpu.CompilerParams(
            collective_id=0, has_side_effects=True, vmem_limit_bytes=60 * 1024 * 1024
        ),
    )(
        tokens,
        expert_ids.T,
        route_scores.T,
        up_weight,
        down_weight,
        latent_weight.T,
        latent_norm_gain.reshape(1, LATENT),
        page_owner,
        jnp.asarray(freq).reshape(1, half),
    )


def solution(mesh):
    placed = (
        P("ep", "dec"),
        P("ep", None),
        P("ep", None),
        P("ep", "dec", None),
        P("ep", None, "dec"),
        P("dec", None),
        P(),
        P("ep"),
    )
    return jax.shard_map(
        on_device,
        mesh=mesh,
        in_specs=placed,
        out_specs=(P("ep", "dec"), P(("ep", "dec"), None)),
        check_vma=False,
    )
```
